32 devices in a mesh: gz: 32 (over z, y, x, core).
Axes of the slice: x: 2, y: 2, z: 4, core: 2. Of those that a mesh axis runs over, the one named last changes fastest.
Arguments:
- order_param: float32 [32, 512, 512], P('gz'), may hold values from 0.05 to 0.95
- concentration: float32 [32, 512, 512], P('gz'), may hold values from 0 to 1
- strain: float32 [6, 32, 512, 512], P(None, 'gz'), may hold values from -6 to 6
- grain_ids: int32 [32, 512, 512], P('gz'), may hold values from 0 to 15
- seed_labels: int32 [32, 512, 512], P('gz'), may hold values from 0 to 8
- grain_moduli: float32 [2, 16], replicated, may hold values from 0.5 to 2
- grain_mobility: float32 [16], replicated, may hold values from 0.25 to 1
- seed_rate: float32 [8], replicated, may hold values from 0.5 to 4
Outputs:
- order_next: float32 [32, 512, 512], P('gz')
- conc_next: float32 [32, 512, 512], P('gz')
- strain_next: float32 [6, 32, 512, 512], P(None, 'gz')
The draws below stay inside these ranges and needn't reach their ends.
Inputs may be any that keep to these rules, and one draw needn't show every extreme that they name: `seed_labels`: 0 marks a voxel without seed; label k > 0 names entry k - 1 of seed_rate.
All inputs are finite; a program needn't handle non-finite values.
Results may differ from the reference program's by a relative error of at most 0.0003.
Values sent between devices are 32-bit elements; how exact they have to be, the bound alone decides.
A program may use at most 256 MiB of HBM per device.

```python
import math
import jax
import jax.numpy as jnp
from jax import lax

NX = 512
NY = 512
GRAINS = 16
SEEDS = 8
SUBSTEPS = 2
NZ = 32


def touch_ends(values, own_key, least, largest):
    longest = values.shape.index(max(values.shape))
    spots = []
    for shift in (0, 1):
        where = [jax.random.randint(jax.random.fold_in(own_key, axis), (), 0, length) for axis, length in enumerate(values.shape)]
        where[longest] = (where[longest] + shift) % values.shape[longest]
        spots.append(tuple(where))
    return values.at[spots[0]].set(least).at[spots[1]].set(largest)


def shard_levels(rng, shape, pieces, least, largest):
    def one(dim, blocks):
        heights = jax.random.uniform(jax.random.fold_in(jax.random.fold_in(rng, 6), dim), (blocks,), jnp.float32, least / len(pieces), largest / len(pieces))
        return jnp.repeat(jnp.exp(heights), shape[dim] // blocks).reshape((-1,) + (1,) * (len(shape) - dim - 1))

    loudness = one(*pieces[0])
    for cut in pieces[1:]:
        loudness = loudness * one(*cut)
    return loudness


def noise(rng, shape, spread, bound, split=(), kind=jnp.bfloat16):
    array = spread * jax.random.normal(rng, shape, jnp.float32)
    if split:
        array = array * shard_levels(rng, shape, split, -0.22, 0.18)
    return jnp.clip(array, -bound, bound).astype(kind)


def setup_inputs(seed: int = 0) -> dict:
    splits = jax.random.split(jax.random.key(seed), 9)
    order_param = jnp.clip(0.05 + 0.9 * jax.random.uniform(splits[0], (NZ, NY, NX), jnp.float32) ** shard_levels(splits[0], (NZ, NY, NX), ((0, 32),), -0.2, 0.2), 0.05, 0.95)
    concentration = jnp.clip(1.0 * jax.random.uniform(splits[1], (NZ, NY, NX), jnp.float32) ** shard_levels(splits[1], (NZ, NY, NX), ((0, 32),), -0.2, 0.2), 0.0, 1.0)
    strain = noise(splits[2], (6, NZ, NY, NX), 1.0, 6.0, ((1, 32),), jnp.float32)
    grain_ids = touch_ends(jax.random.randint(splits[3], (NZ, NY, NX), 0, GRAINS), jax.random.fold_in(splits[3], 1), 0, GRAINS - 1).astype(jnp.int32)
    seed_labels = touch_ends(jax.random.randint(splits[4], (NZ, NY, NX), 0, SEEDS + 1), jax.random.fold_in(splits[4], 1), 0, SEEDS).astype(jnp.int32)
    grain_moduli = jnp.clip(jnp.exp(jax.random.uniform(splits[5], (2, GRAINS), jnp.float32, math.log(0.5), math.log(2.0))), 0.5, 2.0)
    grain_mobility = jnp.clip(jnp.exp(jax.random.uniform(splits[6], (GRAINS,), jnp.float32, math.log(0.25), math.log(1.0))), 0.25, 1.0)
    seed_rate = jnp.clip(jnp.exp(jax.random.uniform(splits[7], (SEEDS,), jnp.float32, math.log(0.5), math.log(4.0))), 0.5, 4.0)
    return {"order_param": order_param, "concentration": concentration, "strain": strain, "grain_ids": grain_ids, "seed_labels": seed_labels, "grain_moduli": grain_moduli, "grain_mobility": grain_mobility, "seed_rate": seed_rate}


time_step = 0.05
grad_coef = 1.0
well_height = 1.0
drive_coef = 2.0
conc_eq = 0.5
mech_boost = 1.0
diffusivity = 1.0
release_coef = 1.0
residual_stiff = 0.1
lame_ref = 1.0
shear_ref = 1.0
coupling = (lame_ref + shear_ref) / (shear_ref * (lame_ref + 2.0 * shear_ref))


def laplace(field):
    z_sum = jnp.roll(field, 1, 0) + jnp.roll(field, -1, 0)
    y_sum = jnp.roll(field, 1, 1) + jnp.roll(field, -1, 1)
    x_sum = jnp.roll(field, 1, 2) + jnp.roll(field, -1, 2)
    return z_sum + y_sum + x_sum - 6.0 * field


def advance(order_now, conc_now, lap_order, lap_conc, kinetic, decay):
    well_grad = 2.0 * order_now * (1.0 - order_now) * (1.0 - 2.0 * order_now)
    interp_grad = 6.0 * order_now * (1.0 - order_now)
    force = grad_coef * lap_order - well_height * well_grad + drive_coef * interp_grad * (conc_now - conc_eq)
    order_new = order_now + kinetic * force - decay * order_now
    conc_new = conc_now + time_step * diffusivity * lap_conc + release_coef * (order_now - order_new)
    return order_new, conc_new


def coefficients(strain, lame, shear, mobility, rate):
    trace = strain[0] + strain[1] + strain[2]
    square = strain[0] * strain[0] + strain[1] * strain[1] + strain[2] * strain[2] + 2.0 * (strain[3] * strain[3] + strain[4] * strain[4] + strain[5] * strain[5])
    energy = 0.5 * lame * trace * trace + shear * square
    mech = 1.0 + mech_boost * energy / (1.0 + energy)
    kinetic = time_step * mobility * mech
    decay = time_step * rate
    return kinetic, decay


def stress_of(strain, order_now, lame, shear):
    scale = order_now * order_now * (3.0 - 2.0 * order_now) + residual_stiff
    lame_now = scale * lame
    shear_now = scale * shear
    trace = strain[0] + strain[1] + strain[2]
    parts = []
    for comp in range(6):
        if comp < 3:
            parts.append(lame_now * trace + 2.0 * shear_now * strain[comp])
        else:
            parts.append(2.0 * shear_now * strain[comp])
    return jnp.stack(parts)


def green(tau, xi_x, xi_y, xi_z, limit):
    t_xx, t_yy, t_zz, t_yz, t_xz, t_xy = tau
    v_x = t_xx * xi_x + t_xy * xi_y + t_xz * xi_z
    v_y = t_xy * xi_x + t_yy * xi_y + t_yz * xi_z
    v_z = t_xz * xi_x + t_yz * xi_y + t_zz * xi_z
    inner = xi_x * v_x + xi_y * v_y + xi_z * v_z
    wave_sq = xi_x * xi_x + xi_y * xi_y + xi_z * xi_z
    live = (wave_sq > 0.5) & (xi_x < limit)
    safe_sq = jnp.where(live, wave_sq, 1.0)
    first = jnp.where(live, 1.0 / (2.0 * shear_ref * safe_sq), 0.0)
    second = jnp.where(live, coupling / (safe_sq * safe_sq), 0.0)
    xis = (xi_x, xi_y, xi_z)
    vees = (v_x, v_y, v_z)
    pairs = ((0, 0), (1, 1), (2, 2), (1, 2), (0, 2), (0, 1))
    result = []
    for left, right in pairs:
        term = (xis[right] * vees[left] + xis[left] * vees[right]) * first - xis[left] * xis[right] * inner * second
        result.append(term)
    return result


def signed_waves(count):
    index = jnp.arange(count, dtype=jnp.int32)
    return jnp.where(index < count // 2, index, index - count).astype(jnp.float32)


def reference(order_param, concentration, strain, grain_ids, seed_labels, grain_moduli, grain_mobility, seed_rate):
    lame = grain_moduli[0][grain_ids]
    shear = grain_moduli[1][grain_ids]
    mobility = grain_mobility[grain_ids]
    seed_index = jnp.maximum(seed_labels - 1, 0).astype(jnp.int32)
    rate = jnp.where(seed_labels > 0, seed_rate[seed_index], jnp.zeros_like(seed_rate[seed_index]))
    kinetic, decay = coefficients(strain, lame, shear, mobility, rate)
    order_now = order_param
    conc_now = concentration
    for step_index in range(SUBSTEPS):
        order_now, conc_now = advance(order_now, conc_now, laplace(order_now), laplace(conc_now), kinetic, decay)
    stress = stress_of(strain, order_now, lame, shear)
    spectrum = jnp.fft.rfftn(stress, axes=(1, 2, 3))
    xi_z = signed_waves(NZ)
    xi_y = signed_waves(NY)[:, None]
    xi_x = jnp.arange(NX // 2 + 1).astype(jnp.float32)
    limit = float(NX // 2)

    def plane(item):
        tau_plane, wave_z = item
        return jnp.stack(green([tau_plane[comp] for comp in range(6)], xi_x, xi_y, wave_z, limit))

    planes = lax.map(plane, (jnp.moveaxis(spectrum, 1, 0), xi_z))
    increment = jnp.fft.irfftn(jnp.moveaxis(planes, 0, 1), s=(NZ, NY, NX), axes=(1, 2, 3))
    strain_next = strain - increment
    return order_now, conc_now, strain_next
```

```python
import functools
import math

import jax
import jax.numpy as jnp
import numpy as np
from jax import lax
from jax.experimental import pallas as pl
from jax.experimental.pallas import tpu as pltpu
from jax.sharding import PartitionSpec as P

SUBSTEPS = 2
time_step = 0.05
conc_eq = 0.5
residual_stiff = 0.1
lame_ref = 1.0
shear_ref = 1.0
coupling = (lame_ref + shear_ref) / (shear_ref * (lame_ref + 2.0 * shear_ref))
F32 = jnp.float32
BF16 = jnp.bfloat16
LIMIT = 50 * 1024 * 1024


def lookup(labels, table, first):
    out = jnp.zeros(labels.shape, F32)
    for k in range(table.shape[0]):
        out = jnp.where(labels == k + first, table[k], out)
    return out


def neighbours(plane):
    count = lax.axis_size("gz")
    below = lax.ppermute(plane, "gz", [(i, (i + 1) % count) for i in range(count)])
    above = lax.ppermute(plane, "gz", [((i + 1) % count, i) for i in range(count)])
    return below + above


def laplace(plane, z_sum):
    y_sum = jnp.roll(plane, 1, 0) + jnp.roll(plane, -1, 0)
    x_sum = jnp.roll(plane, 1, 1) + jnp.roll(plane, -1, 1)
    return z_sum + y_sum + x_sum - 6.0 * plane


def order_step(p, c, lap, kinetic, decay):
    well = 2.0 * p * (1.0 - p) * (1.0 - 2.0 * p)
    interp = 6.0 * p * (1.0 - p)
    force = lap - well + 2.0 * interp * (c - conc_eq)
    return p + kinetic * force - decay * p


def pair(table):
    table = jnp.asarray(np.asarray(table, np.float32))
    hi = table.astype(BF16)
    return hi, (table - hi.astype(F32)).astype(BF16)


def tables(nx, ny, depth):
    hx, hy = nx // 2, ny // 2
    x = np.arange(hx)[:, None]
    y = np.arange(hy)[None, :]
    fx, ix, fy, iy = [], [], [], []
    for par in range(2):
        kx = 2 * np.arange(hx // 2)[None, :] + par
        ph = 2.0 * np.pi * ((x * kx) % nx) / nx
        fx.append(np.concatenate([np.cos(ph), -np.sin(ph)], 1))
        weight = np.where(kx == 0, 1.0, 2.0) / float(nx * ny * depth)
        ix.append(np.concatenate([np.cos(ph) * weight, -np.sin(ph) * weight], 1).T)
        ky = 2 * np.arange(hy)[:, None] + par
        ph = 2.0 * np.pi * ((ky * y) % ny) / ny
        fy.append(np.concatenate([np.cos(ph), np.sin(ph)], 0))
        iy.append(np.concatenate([np.cos(ph).T, np.sin(ph).T], 0))
    return fx, np.stack(fy), ix, np.stack(iy)


def split(x):
    hi = x.astype(BF16)
    return hi, (x - hi.astype(F32)).astype(BF16)


def dot3(a, b):
    def dot(u, v):
        return jnp.dot(u, v, preferred_element_type=F32)

    return dot(a[0], b[0]) + (dot(a[0], b[1]) + dot(a[1], b[0]))


def waves(par, ny, lanes):
    mx = (2 * lax.broadcasted_iota(jnp.int32, (1, lanes), 1) + par[0]).astype(F32)
    row = 2 * lax.broadcasted_iota(jnp.int32, (ny // 2, 1), 0) + par[1]
    my = jnp.where(row < ny // 2, row, row - ny).astype(F32)
    return mx, my


def forward_kernel(h, e_ref, lt_ref, m2_ref, xh_ref, xl_ref, yh_ref, yl_ref, o0_ref, o1_ref):
    t = pl.program_id(0)
    ny, nx = lt_ref.shape
    hy, hx, lanes = ny // 2, nx // 2, nx // 4
    diag = jnp.where((t == 0) | (t == 2) | (t == 5), 1.0, 0.0).astype(F32)
    s = m2_ref[...] * e_ref[0] + diag * lt_ref[...]
    left, right = s[:, :hx], s[:, hx:]
    folded = left + right if h == 0 else left - right
    xs = dot3(split(folded), (xh_ref[...], xl_ref[...]))
    for g, o_ref in enumerate((o0_ref, o1_ref)):
        nd, _, band, _ = o_ref.shape
        ys = xs[:hy] + xs[hy:] if g == 0 else xs[:hy] - xs[hy:]
        d = dot3((yh_ref[g], yl_ref[g]), split(ys))
        re = d[:hy, :lanes] + d[hy:, lanes:]
        im = d[:hy, lanes:] - d[hy:, :lanes]
        mx, my = waves((h, g), ny, lanes)

        def put(slot, a, b, add=False):
            a, b = a.reshape(nd, band, lanes), b.reshape(nd, band, lanes)
            if add:
                a, b = a + o_ref[:, slot], b + o_ref[:, slot + 1]
            o_ref[:, slot] = a
            o_ref[:, slot + 1] = b

        @pl.when(t == 0)
        def _():
            put(0, mx * re, mx * im)

        @pl.when(t == 1)
        def _():
            put(0, my * re, my * im, True)
            put(2, mx * re, mx * im)

        @pl.when(t == 2)
        def _():
            put(2, my * re, my * im, True)

        for k in range(3):
            @pl.when(t == 3 + k)
            def _():
                put(4 + 2 * k, re, im)


def whole(shape):
    return pl.BlockSpec(shape, lambda t: (0,) * len(shape))


def forward(h, strain, lt, m2, fx, fy, devices):
    ny, nx = lt.shape
    shape = (devices, 10, ny // 2 // devices, nx // 4)

    def comp(t):
        c = jnp.where(t == 1, 5, jnp.where(t == 2, 1, jnp.where(t >= 3, 7 - t, 0)))
        return (c, 0, 0)

    return pl.pallas_call(
        functools.partial(forward_kernel, h),
        grid=(6,),
        in_specs=[pl.BlockSpec((1, ny, nx), comp), whole((ny, nx)), whole((ny, nx))]
        + [whole(v.shape) for v in fx + fy],
        out_specs=[whole(shape)] * 2,
        out_shape=[jax.ShapeDtypeStruct(shape, F32)] * 2,
        compiler_params=pltpu.CompilerParams(vmem_limit_bytes=LIMIT),
        cost_estimate=pl.CostEstimate(
            flops=6 * 3 * 2 * (ny * nx * nx // 4 + ny * ny * nx // 2),
            bytes_accessed=14 * 1024 * 1024,
            transcendentals=0,
        ),
    )(strain, lt, m2, *fx, *fy)


def fft(re, im, sign):
    n = len(re)
    if n == 1:
        return re, im
    half = n // 2
    sr = [re[k] + re[k + half] for k in range(half)]
    si = [im[k] + im[k + half] for k in range(half)]
    dr, di = [], []
    for k in range(half):
        a, b = re[k] - re[k + half], im[k] - im[k + half]
        if k == 0:
            dr.append(a)
            di.append(b)
        elif 4 * k == n:
            dr.append(-sign * b)
            di.append(sign * a)
        else:
            c = math.cos(2.0 * math.pi * k / n)
            s = sign * math.sin(2.0 * math.pi * k / n)
            dr.append(a * c - b * s)
            di.append(a * s + b * c)
    er, ei = fft(sr, si, sign)
    orr, oi = fft(dr, di, sign)
    outr, outi = [None] * n, [None] * n
    outr[0::2], outr[1::2], outi[0::2], outi[1::2] = er, orr, ei, oi
    return outr, outi


def green_kernel(h, x_ref, my_ref, o_ref, v_ref):
    depth, _, band, lanes = x_ref.shape

    def transform(src, dst, sign):
        def body(c, carry):
            re = [src[k, 2 * c] for k in range(depth)]
            im = [src[k, 2 * c + 1] for k in range(depth)]
            re, im = fft(re, im, sign)
            for k in range(depth):
                dst[k, 2 * c] = re[k]
                dst[k, 2 * c + 1] = im[k]
            return carry

        lax.fori_loop(0, 5, body, 0)

    transform(x_ref, v_ref, -1.0)
    mx = (2 * lax.broadcasted_iota(jnp.int32, (band, lanes), 1) + h).astype(F32)
    my = my_ref[...]
    flat = mx * mx + my * my

    def body(k, carry):
        mz = jnp.where(k < depth // 2, k, k - depth).astype(F32)
        k2 = flat + mz * mz
        live = k2 > 0.5
        inv = jnp.where(live, 1.0 / jnp.where(live, k2, 1.0), 0.0)
        for part in range(2):
            wx, wy, txz, tyz, tzz = [v_ref[k, 2 * c + part] for c in range(5)]
            vx = wx + mz * txz
            vy = wy + mz * tyz
            vz = mx * txz + my * tyz + mz * tzz
            inner = (mx * vx + my * vy + mz * vz) * (coupling * inv)
            ux = (vx - mx * inner) * inv
            uy = (vy - my * inner) * inv
            uz = (vz - mz * inner) * inv
            v_ref[k, part] = ux
            v_ref[k, 2 + part] = uy
            v_ref[k, 4 + part] = 0.5 * (mx * uz + mz * ux)
            v_ref[k, 6 + part] = 0.5 * (my * uz + mz * uy)
            v_ref[k, 8 + part] = mz * uz
        return carry

    lax.fori_loop(0, depth, body, 0)
    transform(v_ref, o_ref, 1.0)


def green(h, g, chunk, ny):
    depth, _, band, lanes = chunk.shape
    row = 2 * (lax.axis_index("gz") * band + jnp.arange(band, dtype=jnp.int32)) + g
    my = jnp.where(row < ny // 2, row, row - ny).astype(F32)
    my = jnp.broadcast_to(my[:, None], (band, lanes))
    return pl.pallas_call(
        functools.partial(green_kernel, h),
        in_specs=[pl.BlockSpec(memory_space=pltpu.VMEM)] * 2,
        out_specs=pl.BlockSpec(memory_space=pltpu.VMEM),
        out_shape=jax.ShapeDtypeStruct(chunk.shape, F32),
        scratch_shapes=[pltpu.VMEM(chunk.shape, F32)],
        compiler_params=pltpu.CompilerParams(vmem_limit_bytes=LIMIT),
        cost_estimate=pl.CostEstimate(
            flops=chunk.size * 64, bytes_accessed=chunk.size * 8, transcendentals=0
        ),
    )(chunk, my)


def inverse_kernel(h, r0_ref, r1_ref, xh_ref, xl_ref, yh_ref, yl_ref, *rest):
    g_ref = rest[-1]
    t = pl.program_id(0)
    lanes = r0_ref.shape[3]
    hy = r0_ref.shape[0] * r0_ref.shape[2]
    sums = []
    for g, r_ref in enumerate((r0_ref, r1_ref)):
        mx, my = waves((h, g), 2 * hy, lanes)

        def get(slot):
            return [r_ref[:, slot + part].reshape(hy, lanes) for part in range(2)]

        def put(a, b):
            g_ref[:, :lanes] = a
            g_ref[:, lanes:] = b

        @pl.when(t == 0)
        def _():
            a, b = get(0)
            put(mx * a, mx * b)

        @pl.when(t == 1)
        def _():
            a, b = get(2)
            put(my * a, my * b)

        @pl.when(t == 5)
        def _():
            a, b = get(0)
            c, d = get(2)
            put(0.5 * (my * a + mx * c), 0.5 * (my * b + mx * d))

        @pl.when((t >= 2) & (t <= 4))
        def _():
            put(*get(2 * (6 - t)))

        d = dot3((yh_ref[g], yl_ref[g]), split(g_ref[...]))
        re = d[:hy, :lanes] - d[hy:, lanes:]
        im = d[:hy, lanes:] + d[hy:, :lanes]
        sums.append(jnp.concatenate([re, im], axis=1))
    full = jnp.concatenate([sums[0] + sums[1], sums[0] - sums[1]], axis=0)
    z = dot3(split(full), (xh_ref[...], xl_ref[...]))
    if h == 0:
        rest[0][0] = z
    else:
        z0_ref, e_ref, o_ref = rest[:3]
        hx = z.shape[1]
        z0 = z0_ref[0]
        o_ref[0, :, :hx] = e_ref[0, :, :hx] - (z0 + z)
        o_ref[0, :, hx:] = e_ref[0, :, hx:] - (z0 - z)


def inverse(h, r0, r1, ix, iy, ny, nx, extra=()):
    def plane(width):
        return pl.BlockSpec((1, ny, width), lambda t: (t, 0, 0))

    width = nx // 2 if h == 0 else nx
    return pl.pallas_call(
        functools.partial(inverse_kernel, h),
        grid=(6,),
        in_specs=[whole(v.shape) for v in (r0, r1) + ix + iy]
        + [plane(v.shape[2]) for v in extra],
        out_specs=plane(width),
        out_shape=jax.ShapeDtypeStruct((6, ny, width), F32),
        scratch_shapes=[pltpu.VMEM((ny // 2, nx // 2), F32)],
        compiler_params=pltpu.CompilerParams(vmem_limit_bytes=LIMIT),
        cost_estimate=pl.CostEstimate(
            flops=6 * 3 * 2 * (ny * nx * nx // 4 + ny * ny * nx // 2),
            bytes_accessed=14 * 1024 * 1024,
            transcendentals=0,
        ),
    )(r0, r1, *ix, *iy, *extra)


def shards(
    order_param,
    concentration,
    strain,
    grain_ids,
    seed_labels,
    grain_moduli,
    grain_mobility,
    seed_rate,
):
    devices = lax.axis_size("gz")
    ny, nx = strain.shape[2], strain.shape[3]
    fx, fy, ix, iy = tables(nx, ny, devices)
    fx, ix = [pair(v) for v in fx], [pair(v) for v in ix]
    fy, iy = pair(fy), pair(iy)
    strain = strain.reshape(6, ny, nx)
    p, c = order_param[0], concentration[0]
    p_sum = neighbours(p)
    c_sum = neighbours(c)
    ids, seeds = grain_ids[0], seed_labels[0]
    lame = lookup(ids, grain_moduli[0], 0)
    shear = lookup(ids, grain_moduli[1], 0)
    mobility = lookup(ids, grain_mobility, 0)
    rate = lookup(seeds, seed_rate, 1)
    trace = strain[0] + strain[1] + strain[2]
    square = (
        strain[0] * strain[0]
        + strain[1] * strain[1]
        + strain[2] * strain[2]
        + 2.0 * (strain[3] * strain[3] + strain[4] * strain[4] + strain[5] * strain[5])
    )
    energy = 0.5 * lame * trace * trace + shear * square
    kinetic = time_step * mobility * (1.0 + energy / (1.0 + energy))
    decay = time_step * rate
    p1 = order_step(p, c, laplace(p, p_sum), kinetic, decay)
    p1_sum = neighbours(p1)
    c1 = c + time_step * laplace(c, c_sum) + (p - p1)
    p2 = order_step(p1, c1, laplace(p1, p1_sum), kinetic, decay)
    scale = p2 * p2 * (3.0 - 2.0 * p2) + residual_stiff
    lt = scale * lame * trace
    m2 = 2.0 * (scale * shear)

    sent = [list(forward(h, strain, lt, m2, fx[h], fy, devices)) for h in range(2)]
    c1_late, sent[0][0] = lax.optimization_barrier((c1, sent[0][0]))
    c1_sum = neighbours(c1_late)
    c2 = c1_late + time_step * laplace(c1_late, c1_sum) + (p1 - p2)

    def swap(chunk):
        return lax.all_to_all(chunk, "gz", split_axis=0, concat_axis=0, tiled=True)

    back = [[swap(green(h, g, swap(sent[h][g]), ny)) for g in range(2)] for h in range(2)]
    z0 = inverse(0, back[0][0], back[0][1], ix[0], iy, ny, nx)
    out = inverse(1, back[1][0], back[1][1], ix[1], iy, ny, nx, (z0, strain))
    return (p2[None], c2[None], out[:, None])


def solution(mesh):
    return jax.shard_map(
        shards,
        mesh=mesh,
        in_specs=(
            P("gz", None, None),
            P("gz", None, None),
            P(None, "gz", None, None),
            P("gz", None, None),
            P("gz", None, None),
            P(),
            P(),
            P(),
        ),
        out_specs=(P("gz", None, None), P("gz", None, None), P(None, "gz", None, None)),
        check_vma=False,
    )
```

```python
import functools
import math

import jax
import jax.numpy as jnp
import numpy as np
from jax import lax
from jax.experimental import pallas as pl
from jax.experimental.pallas import tpu as pltpu
from jax.sharding import PartitionSpec as P

SUBSTEPS = 2
time_step = 0.05
conc_eq = 0.5
residual_stiff = 0.1
lame_ref = 1.0
shear_ref = 1.0
coupling = (lame_ref + shear_ref) / (shear_ref * (lame_ref + 2.0 * shear_ref))
F32 = jnp.float32
BF16 = jnp.bfloat16
LIMIT = 50 * 1024 * 1024


def neighbours(plane):
    count = lax.axis_size("gz")
    below = lax.ppermute(plane, "gz", [(i, (i + 1) % count) for i in range(count)])
    above = lax.ppermute(plane, "gz", [((i + 1) % count, i) for i in range(count)])
    return below, above


def laplace_plane(plane):
    ny, nx = plane.shape
    y_sum = pltpu.roll(plane, 1, 0) + pltpu.roll(plane, ny - 1, 0)
    x_sum = pltpu.roll(plane, 1, 1) + pltpu.roll(plane, nx - 1, 1)
    return y_sum + x_sum - 6.0 * plane


def order_part(p, c, kinetic, decay):
    well = 2.0 * p * (1.0 - p) * (1.0 - 2.0 * p)
    interp = 6.0 * p * (1.0 - p)
    force = laplace_plane(p) - well + 2.0 * interp * (c - conc_eq)
    return p + kinetic * force - decay * p


def local_kernel(
    moduli_ref, mobility_ref, rate_ref, p_ref, c_ref, e_ref, ids_ref, seeds_ref,
    lt_ref, m2_ref, kin_ref, dec_ref, pa_ref, ca_ref,
):
    rows = 8

    def body(k, carry):
        at = pl.ds(pl.multiple_of(k * rows, rows), rows)
        ids, seeds = ids_ref[at, :], seeds_ref[at, :]
        lame = jnp.zeros(ids.shape, F32)
        shear, mobility, rate = lame, lame, lame
        for n in range(mobility_ref.shape[0]):
            hit = ids == n
            lame = jnp.where(hit, moduli_ref[0, n], lame)
            shear = jnp.where(hit, moduli_ref[1, n], shear)
            mobility = jnp.where(hit, mobility_ref[n], mobility)
        for n in range(rate_ref.shape[0]):
            rate = jnp.where(seeds == n + 1, rate_ref[n], rate)
        e = [e_ref[n, at, :] for n in range(6)]
        trace = e[0] + e[1] + e[2]
        square = (
            e[0] * e[0] + e[1] * e[1] + e[2] * e[2]
            + 2.0 * (e[3] * e[3] + e[4] * e[4] + e[5] * e[5])
        )
        energy = 0.5 * lame * trace * trace + shear * square
        kin_ref[at, :] = time_step * mobility * (1.0 + energy / (1.0 + energy))
        dec_ref[at, :] = time_step * rate
        lt_ref[at, :] = lame * trace
        m2_ref[at, :] = 2.0 * shear
        return carry

    lax.fori_loop(0, p_ref.shape[0] // rows, body, 0)
    p, c = p_ref[...], c_ref[...]
    pa_ref[...] = order_part(p, c, kin_ref[...], dec_ref[...])
    ca_ref[...] = c + time_step * laplace_plane(c) + p


def second_kernel(p1_ref, ca_ref, cb_ref, cu_ref, kin_ref, dec_ref, c1_ref, pa_ref, cc_ref):
    p1 = p1_ref[...]
    c1_ref[...] = ca_ref[...] + time_step * (cb_ref[...] + cu_ref[...]) - p1
    pa_ref[...] = order_part(p1, c1_ref[...], kin_ref[...], dec_ref[...])
    c1 = c1_ref[...]
    cc_ref[...] = c1 + time_step * laplace_plane(c1) + p1


def planes_call(kernel, scalars, arrays, outs):
    shape = arrays[0].shape
    total = sum(v.size * 4 for v in arrays) + outs * 4 * arrays[0].size
    return pl.pallas_call(
        kernel,
        in_specs=[pl.BlockSpec(memory_space=pltpu.SMEM)] * len(scalars)
        + [pl.BlockSpec(memory_space=pltpu.VMEM)] * len(arrays),
        out_specs=[pl.BlockSpec(memory_space=pltpu.VMEM)] * outs,
        out_shape=[jax.ShapeDtypeStruct(shape, F32)] * outs,
        compiler_params=pltpu.CompilerParams(vmem_limit_bytes=LIMIT),
        cost_estimate=pl.CostEstimate(flops=100 * total, bytes_accessed=total, transcendentals=0),
    )(*scalars, *arrays)


def pair(table):
    table = jnp.asarray(np.asarray(table, np.float32))
    hi = table.astype(BF16)
    return hi, (table - hi.astype(F32)).astype(BF16)


def tables(nx, ny, depth):
    hx, hy = nx // 2, ny // 2
    x = np.arange(hx)[:, None]
    y = np.arange(hy)[None, :]
    fx, ix, fy, iy = [], [], [], []
    for par in range(2):
        kx = 2 * np.arange(hx // 2)[None, :] + par
        ph = 2.0 * np.pi * ((x * kx) % nx) / nx
        fx.append(np.concatenate([np.cos(ph), -np.sin(ph)], 1))
        weight = np.where(kx == 0, 1.0, 2.0) / float(nx * ny * depth)
        ix.append(np.concatenate([np.cos(ph) * weight, -np.sin(ph) * weight], 1).T)
        ky = 2 * np.arange(hy)[:, None] + par
        ph = 2.0 * np.pi * ((ky * y) % ny) / ny
        fy.append(np.concatenate([np.cos(ph), np.sin(ph)], 0))
        iy.append(np.concatenate([np.cos(ph).T, np.sin(ph).T], 0))
    return fx, np.stack(fy), ix, np.stack(iy)


def split(x):
    hi = x.astype(BF16)
    return hi, (x - hi.astype(F32)).astype(BF16)


def dot3(a, b):
    def dot(u, v):
        return jnp.dot(u, v, preferred_element_type=F32)

    return dot(a[0], b[0]) + (dot(a[0], b[1]) + dot(a[1], b[0]))


def waves(par, ny, lanes):
    mx = (2 * lax.broadcasted_iota(jnp.int32, (1, lanes), 1) + par[0]).astype(F32)
    row = 2 * lax.broadcasted_iota(jnp.int32, (ny // 2, 1), 0) + par[1]
    my = jnp.where(row < ny // 2, row, row - ny).astype(F32)
    return mx, my


def forward_kernel(h, e_ref, lt_ref, m2_ref, xh_ref, xl_ref, yh_ref, yl_ref, *rest):
    t = pl.program_id(0)
    scale_ref = rest[-1]

    @pl.when(t == 0)
    def _():
        if h == 0:
            pa_ref, kin_ref, pb_ref, pu_ref, _, p_ref, _ = rest
            p_ref[...] = pa_ref[...] + kin_ref[...] * (pb_ref[...] + pu_ref[...])
        else:
            p_ref = rest[0]
        p = p_ref[...]
        scale_ref[...] = p * p * (3.0 - 2.0 * p) + residual_stiff

    o_ref = rest[4] if h == 0 else rest[1]
    nd, _, band, _ = o_ref.shape
    ny, nx = lt_ref.shape
    hy, hx, lanes = ny // 2, nx // 2, nx // 4
    diag = jnp.where((t == 0) | (t == 2) | (t == 5), 1.0, 0.0).astype(F32)
    s = scale_ref[...] * (m2_ref[...] * e_ref[0] + diag * lt_ref[...])
    left, right = s[:, :hx], s[:, hx:]
    folded = left + right if h == 0 else left - right
    xs = dot3(split(folded), (xh_ref[...], xl_ref[...]))
    for g in range(2):
        ys = xs[:hy] + xs[hy:] if g == 0 else xs[:hy] - xs[hy:]
        d = dot3((yh_ref[g], yl_ref[g]), split(ys))
        re = d[:hy, :lanes] + d[hy:, lanes:]
        im = d[:hy, lanes:] - d[hy:, :lanes]
        mx, my = waves((h, g), ny, lanes)

        def put(slot, a, b, add=False, base=10 * g):
            slot = slot + base
            a, b = a.reshape(nd, band, lanes), b.reshape(nd, band, lanes)
            if add:
                a, b = a + o_ref[:, slot], b + o_ref[:, slot + 1]
            o_ref[:, slot] = a
            o_ref[:, slot + 1] = b

        @pl.when(t == 0)
        def _():
            put(0, mx * re, mx * im)

        @pl.when(t == 1)
        def _():
            put(0, my * re, my * im, True)
            put(2, mx * re, mx * im)

        @pl.when(t == 2)
        def _():
            put(2, my * re, my * im, True)

        for k in range(3):
            @pl.when(t == 3 + k)
            def _():
                put(4 + 2 * k, re, im)


def whole(shape):
    return pl.BlockSpec(shape, lambda t: (0,) * len(shape))


def forward(h, strain, lt, m2, fx, fy, devices, more):
    ny, nx = lt.shape
    shape = (devices, 20, ny // 2 // devices, nx // 4)
    shapes = [shape, (ny, nx)] if h == 0 else [shape]

    def comp(t):
        c = jnp.where(t == 1, 5, jnp.where(t == 2, 1, jnp.where(t >= 3, 7 - t, 0)))
        return (c, 0, 0)

    return pl.pallas_call(
        functools.partial(forward_kernel, h),
        grid=(6,),
        in_specs=[pl.BlockSpec((1, ny, nx), comp), whole((ny, nx)), whole((ny, nx))]
        + [whole(v.shape) for v in fx + fy + more],
        out_specs=[whole(v) for v in shapes],
        out_shape=[jax.ShapeDtypeStruct(v, F32) for v in shapes],
        scratch_shapes=[pltpu.VMEM((ny, nx), F32)],
        compiler_params=pltpu.CompilerParams(vmem_limit_bytes=LIMIT),
        cost_estimate=pl.CostEstimate(
            flops=6 * 3 * 2 * (ny * nx * nx // 4 + ny * ny * nx // 2),
            bytes_accessed=14 * 1024 * 1024,
            transcendentals=0,
        ),
    )(strain, lt, m2, *fx, *fy, *more)


def fft(re, im, sign):
    n = len(re)
    if n == 1:
        return re, im
    half = n // 2
    sr = [re[k] + re[k + half] for k in range(half)]
    si = [im[k] + im[k + half] for k in range(half)]
    dr, di = [], []
    for k in range(half):
        a, b = re[k] - re[k + half], im[k] - im[k + half]
        if k == 0:
            dr.append(a)
            di.append(b)
        elif 4 * k == n:
            dr.append(-sign * b)
            di.append(sign * a)
        else:
            c = math.cos(2.0 * math.pi * k / n)
            s = sign * math.sin(2.0 * math.pi * k / n)
            dr.append(a * c - b * s)
            di.append(a * s + b * c)
    er, ei = fft(sr, si, sign)
    orr, oi = fft(dr, di, sign)
    outr, outi = [None] * n, [None] * n
    outr[0::2], outr[1::2], outi[0::2], outi[1::2] = er, orr, ei, oi
    return outr, outi


def green_kernel(h, x_ref, my_ref, o_ref, v_ref):
    depth, _, band, lanes = x_ref.shape

    def transform(src, dst, sign):
        def body(c, carry):
            re = [src[k, 2 * c] for k in range(depth)]
            im = [src[k, 2 * c + 1] for k in range(depth)]
            re, im = fft(re, im, sign)
            for k in range(depth):
                dst[k, 2 * c] = re[k]
                dst[k, 2 * c + 1] = im[k]
            return carry

        lax.fori_loop(0, x_ref.shape[1] // 2, body, 0)

    transform(x_ref, v_ref, -1.0)
    mx = (2 * lax.broadcasted_iota(jnp.int32, (band, lanes), 1) + h).astype(F32)

    def body(k, carry):
        mz = jnp.where(k < depth // 2, k, k - depth).astype(F32)
        for g in range(2):
            my = my_ref[g]
            k2 = mx * mx + my * my + mz * mz
            live = k2 > 0.5
            inv = jnp.where(live, 1.0 / jnp.where(live, k2, 1.0), 0.0)
            for part in range(2):
                at = 10 * g + part
                wx, wy, txz, tyz, tzz = [v_ref[k, at + 2 * c] for c in range(5)]
                vx = wx + mz * txz
                vy = wy + mz * tyz
                vz = mx * txz + my * tyz + mz * tzz
                inner = (mx * vx + my * vy + mz * vz) * (coupling * inv)
                ux = (vx - mx * inner) * inv
                uy = (vy - my * inner) * inv
                uz = (vz - mz * inner) * inv
                v_ref[k, at] = ux
                v_ref[k, at + 2] = uy
                v_ref[k, at + 4] = 0.5 * (mx * uz + mz * ux)
                v_ref[k, at + 6] = 0.5 * (my * uz + mz * uy)
                v_ref[k, at + 8] = mz * uz
        return carry

    lax.fori_loop(0, depth, body, 0)
    transform(v_ref, o_ref, 1.0)


def green(h, chunk, ny):
    depth, _, band, lanes = chunk.shape
    row = 2 * (lax.axis_index("gz") * band + jnp.arange(band, dtype=jnp.int32))
    row = row[None] + jnp.arange(2, dtype=jnp.int32)[:, None]
    my = jnp.where(row < ny // 2, row, row - ny).astype(F32)
    my = jnp.broadcast_to(my[:, :, None], (2, band, lanes))
    return pl.pallas_call(
        functools.partial(green_kernel, h),
        in_specs=[pl.BlockSpec(memory_space=pltpu.VMEM)] * 2,
        out_specs=pl.BlockSpec(memory_space=pltpu.VMEM),
        out_shape=jax.ShapeDtypeStruct(chunk.shape, F32),
        scratch_shapes=[pltpu.VMEM(chunk.shape, F32)],
        compiler_params=pltpu.CompilerParams(vmem_limit_bytes=LIMIT),
        cost_estimate=pl.CostEstimate(
            flops=chunk.size * 64, bytes_accessed=chunk.size * 8, transcendentals=0
        ),
    )(chunk, my)


def inverse_kernel(h, r_ref, xh_ref, xl_ref, yh_ref, yl_ref, *rest):
    g_ref = rest[-1]
    t = pl.program_id(0)
    lanes = r_ref.shape[3]
    hy = r_ref.shape[0] * r_ref.shape[2]
    sums = []
    for g in range(2):
        mx, my = waves((h, g), 2 * hy, lanes)

        def get(slot, base=10 * g):
            slot = slot + base
            return [r_ref[:, slot + part].reshape(hy, lanes) for part in range(2)]

        def put(a, b):
            g_ref[:, :lanes] = a
            g_ref[:, lanes:] = b

        @pl.when(t == 0)
        def _():
            a, b = get(0)
            put(mx * a, mx * b)

        @pl.when(t == 1)
        def _():
            a, b = get(2)
            put(my * a, my * b)

        @pl.when(t == 5)
        def _():
            a, b = get(0)
            c, d = get(2)
            put(0.5 * (my * a + mx * c), 0.5 * (my * b + mx * d))

        @pl.when((t >= 2) & (t <= 4))
        def _():
            put(*get(2 * (6 - t)))

        d = dot3((yh_ref[g], yl_ref[g]), split(g_ref[...]))
        re = d[:hy, :lanes] - d[hy:, lanes:]
        im = d[:hy, lanes:] + d[hy:, :lanes]
        sums.append(jnp.concatenate([re, im], axis=1))
    full = jnp.concatenate([sums[0] + sums[1], sums[0] - sums[1]], axis=0)
    z = dot3(split(full), (xh_ref[...], xl_ref[...]))
    if h == 0:
        rest[0][0] = z
    else:
        z0_ref, e_ref, o_ref = rest[:3]
        hx = z.shape[1]
        z0 = z0_ref[0]
        o_ref[0, :, :hx] = e_ref[0, :, :hx] - (z0 + z)
        o_ref[0, :, hx:] = e_ref[0, :, hx:] - (z0 - z)


def inverse(h, r, ix, iy, ny, nx, extra=()):
    def plane(width):
        return pl.BlockSpec((1, ny, width), lambda t: (t, 0, 0))

    width = nx // 2 if h == 0 else nx
    return pl.pallas_call(
        functools.partial(inverse_kernel, h),
        grid=(6,),
        in_specs=[whole(v.shape) for v in (r,) + ix + iy]
        + [plane(v.shape[2]) for v in extra],
        out_specs=plane(width),
        out_shape=jax.ShapeDtypeStruct((6, ny, width), F32),
        scratch_shapes=[pltpu.VMEM((ny // 2, nx // 2), F32)],
        compiler_params=pltpu.CompilerParams(vmem_limit_bytes=LIMIT),
        cost_estimate=pl.CostEstimate(
            flops=6 * 3 * 2 * (ny * nx * nx // 4 + ny * ny * nx // 2),
            bytes_accessed=14 * 1024 * 1024,
            transcendentals=0,
        ),
    )(r, *ix, *iy, *extra)


def shards(
    order_param,
    concentration,
    strain,
    grain_ids,
    seed_labels,
    grain_moduli,
    grain_mobility,
    seed_rate,
):
    devices = lax.axis_size("gz")
    ny, nx = strain.shape[2], strain.shape[3]
    fx, fy, ix, iy = tables(nx, ny, devices)
    fx, ix = [pair(v) for v in fx], [pair(v) for v in ix]
    fy, iy = pair(fy), pair(iy)
    strain = strain.reshape(6, ny, nx)
    p, c = order_param[0], concentration[0]
    p_halo = neighbours(p)
    c_halo = neighbours(c)
    lt, m2, kinetic, decay, p_part, c_part = planes_call(
        local_kernel,
        (grain_moduli, grain_mobility, seed_rate),
        (p, c, strain, grain_ids[0], seed_labels[0]),
        6,
    )
    p1 = p_part + kinetic * (p_halo[0] + p_halo[1])
    p1_halo = neighbours(p1)
    c1, p2_part, c2_part = planes_call(
        second_kernel, (), (p1, c_part, *c_halo, kinetic, decay), 3
    )

    def swap(chunk):
        return lax.all_to_all(chunk, "gz", split_axis=0, concat_axis=0, tiled=True)

    sent0, p2 = forward(0, strain, lt, m2, fx[0], fy, devices, (p2_part, kinetic, *p1_halo))
    (sent1,) = forward(1, strain, lt, m2, fx[1], fy, devices, (p2,))
    band0 = swap(sent0)
    band0, c1 = lax.optimization_barrier((band0, c1))
    c1_halo = neighbours(c1)
    band1 = swap(sent1)
    back0 = swap(green(0, band0, ny))
    done1, c1_halo = lax.optimization_barrier((green(1, band1, ny), c1_halo))
    c2 = c2_part + time_step * (c1_halo[0] + c1_halo[1]) - p2
    back1 = swap(done1)
    z0 = inverse(0, back0, ix[0], iy, ny, nx)
    out = inverse(1, back1, ix[1], iy, ny, nx, (z0, strain))
    return (p2[None], c2[None], out[:, None])


def solution(mesh):
    return jax.shard_map(
        shards,
        mesh=mesh,
        in_specs=(
            P("gz", None, None),
            P("gz", None, None),
            P(None, "gz", None, None),
            P("gz", None, None),
            P("gz", None, None),
            P(),
            P(),
            P(),
        ),
        out_specs=(P("gz", None, None), P("gz", None, None), P(None, "gz", None, None)),
        check_vma=False,
    )
```

```python
import functools
import math

import jax
import jax.numpy as jnp
import ml_dtypes
import numpy as np
from jax import lax
from jax.experimental import pallas as pl
from jax.experimental.pallas import tpu as pltpu
from jax.sharding import PartitionSpec as P

SUBSTEPS = 2
time_step = 0.05
conc_eq = 0.5
residual_stiff = 0.1
lame_ref = 1.0
shear_ref = 1.0
coupling = (lame_ref + shear_ref) / (shear_ref * (lame_ref + 2.0 * shear_ref))
F32 = jnp.float32
BF16 = jnp.bfloat16
LIMIT = 50 * 1024 * 1024


def neighbours(plane):
    count = lax.axis_size("gz")
    below = lax.ppermute(plane, "gz", [(i, (i + 1) % count) for i in range(count)])
    above = lax.ppermute(plane, "gz", [((i + 1) % count, i) for i in range(count)])
    return below, above


def laplace_plane(plane):
    ny, nx = plane.shape
    y_sum = pltpu.roll(plane, 1, 0) + pltpu.roll(plane, ny - 1, 0)
    x_sum = pltpu.roll(plane, 1, 1) + pltpu.roll(plane, nx - 1, 1)
    return y_sum + x_sum - 6.0 * plane


def order_part(p, c, kinetic, decay):
    well = 2.0 * p * (1.0 - p) * (1.0 - 2.0 * p)
    interp = 6.0 * p * (1.0 - p)
    force = laplace_plane(p) - well + 2.0 * interp * (c - conc_eq)
    return p + kinetic * force - decay * p


def local_kernel(
    moduli_ref, mobility_ref, rate_ref, p_ref, c_ref, e_ref, ids_ref, seeds_ref,
    lt_ref, m2_ref, kin_ref, dec_ref, pa_ref, ca_ref,
):
    rows = 8

    def body(k, carry):
        at = pl.ds(pl.multiple_of(k * rows, rows), rows)
        ids, seeds = ids_ref[at, :], seeds_ref[at, :]
        lame = jnp.zeros(ids.shape, F32)
        shear, mobility, rate = lame, lame, lame
        for n in range(mobility_ref.shape[0]):
            hit = ids == n
            lame = jnp.where(hit, moduli_ref[0, n], lame)
            shear = jnp.where(hit, moduli_ref[1, n], shear)
            mobility = jnp.where(hit, mobility_ref[n], mobility)
        for n in range(rate_ref.shape[0]):
            rate = jnp.where(seeds == n + 1, rate_ref[n], rate)
        e = [e_ref[n, at, :] for n in range(6)]
        trace = e[0] + e[1] + e[2]
        square = (
            e[0] * e[0] + e[1] * e[1] + e[2] * e[2]
            + 2.0 * (e[3] * e[3] + e[4] * e[4] + e[5] * e[5])
        )
        energy = 0.5 * lame * trace * trace + shear * square
        kin_ref[at, :] = time_step * mobility * (1.0 + energy / (1.0 + energy))
        dec_ref[at, :] = time_step * rate
        lt_ref[at, :] = lame * trace
        m2_ref[at, :] = 2.0 * shear
        return carry

    lax.fori_loop(0, p_ref.shape[0] // rows, body, 0)
    p, c = p_ref[...], c_ref[...]
    pa_ref[...] = order_part(p, c, kin_ref[...], dec_ref[...])
    ca_ref[...] = c + time_step * laplace_plane(c) + p


def second_kernel(p1_ref, ca_ref, cb_ref, cu_ref, kin_ref, dec_ref, c1_ref, pa_ref, cc_ref):
    p1 = p1_ref[...]
    c1_ref[...] = ca_ref[...] + time_step * (cb_ref[...] + cu_ref[...]) - p1
    pa_ref[...] = order_part(p1, c1_ref[...], kin_ref[...], dec_ref[...])
    c1 = c1_ref[...]
    cc_ref[...] = c1 + time_step * laplace_plane(c1) + p1


def planes_call(kernel, scalars, arrays, outs):
    shape = arrays[0].shape
    total = sum(v.size * 4 for v in arrays) + outs * 4 * arrays[0].size
    return pl.pallas_call(
        kernel,
        in_specs=[pl.BlockSpec(memory_space=pltpu.SMEM)] * len(scalars)
        + [pl.BlockSpec(memory_space=pltpu.VMEM)] * len(arrays),
        out_specs=[pl.BlockSpec(memory_space=pltpu.VMEM)] * outs,
        out_shape=[jax.ShapeDtypeStruct(shape, F32)] * outs,
        compiler_params=pltpu.CompilerParams(vmem_limit_bytes=LIMIT),
        cost_estimate=pl.CostEstimate(flops=100 * total, bytes_accessed=total, transcendentals=0),
    )(*scalars, *arrays)


def triple(table, axis, order):
    table = np.asarray(table, np.float32)
    hi = table.astype(ml_dtypes.bfloat16)
    lo = (table - hi.astype(np.float32)).astype(ml_dtypes.bfloat16)
    return jnp.asarray(np.concatenate([(hi, lo)[k] for k in order], axis=axis))


def tables(nx, ny, depth):
    hx, hy = nx // 2, ny // 2
    x = np.arange(hx)[:, None]
    y = np.arange(hy)[None, :]
    fx, ix, fy, iy = [], [], [], []
    for par in range(2):
        kx = 2 * np.arange(hx // 2)[None, :] + par
        ph = 2.0 * np.pi * ((x * kx) % nx) / nx
        fx.append(np.concatenate([np.cos(ph), -np.sin(ph)], 1))
        weight = np.where(kx == 0, 1.0, 2.0) / float(nx * ny * depth)
        ix.append(np.concatenate([np.cos(ph) * weight, -np.sin(ph) * weight], 1).T)
        ky = 2 * np.arange(hy)[:, None] + par
        ph = 2.0 * np.pi * ((ky * y) % ny) / ny
        fy.append(np.concatenate([np.cos(ph), np.sin(ph)], 0))
        iy.append(np.concatenate([np.cos(ph).T, np.sin(ph).T], 0))
    return fx, np.stack(fy), ix, np.stack(iy)


def split(x):
    hi = x.astype(BF16)
    return hi, (x - hi.astype(F32)).astype(BF16)


def dot_right(a, table):
    hi, lo = split(a)
    left = jnp.concatenate([hi, hi, lo], axis=1)
    return jnp.dot(left, table, preferred_element_type=F32)


def dot_left(table, b):
    hi, lo = split(b)
    right = jnp.concatenate([hi, hi, lo], axis=0)
    return jnp.dot(table, right, preferred_element_type=F32)


def waves(par, ny, lanes):
    mx = (2 * lax.broadcasted_iota(jnp.int32, (1, lanes), 1) + par[0]).astype(F32)
    row = 2 * lax.broadcasted_iota(jnp.int32, (ny // 2, 1), 0) + par[1]
    my = jnp.where(row < ny // 2, row, row - ny).astype(F32)
    return mx, my


def forward_kernel(h, e_ref, lt_ref, m2_ref, x_ref, y_ref, *rest):
    t = pl.program_id(0)
    scale_ref = rest[-1]

    @pl.when(t == 0)
    def _():
        if h == 0:
            pa_ref, kin_ref, pb_ref, pu_ref, _, p_ref, _ = rest
            p_ref[...] = pa_ref[...] + kin_ref[...] * (pb_ref[...] + pu_ref[...])
        else:
            p_ref = rest[0]
        p = p_ref[...]
        scale_ref[...] = p * p * (3.0 - 2.0 * p) + residual_stiff

    o_ref = rest[4] if h == 0 else rest[1]
    nd, _, band, _ = o_ref.shape
    ny, nx = lt_ref.shape
    hy, hx, lanes = ny // 2, nx // 2, nx // 4
    diag = jnp.where((t == 0) | (t == 2) | (t == 5), 1.0, 0.0).astype(F32)
    s = scale_ref[...] * (m2_ref[...] * e_ref[0] + diag * lt_ref[...])
    left, right = s[:, :hx], s[:, hx:]
    folded = left + right if h == 0 else left - right
    xs = dot_right(folded, x_ref[...])
    for g in range(2):
        ys = xs[:hy] + xs[hy:] if g == 0 else xs[:hy] - xs[hy:]
        d = dot_left(y_ref[g], ys)
        re = d[:hy, :lanes] + d[hy:, lanes:]
        im = d[:hy, lanes:] - d[hy:, :lanes]
        mx, my = waves((h, g), ny, lanes)

        def put(slot, a, b, add=False, base=10 * g):
            slot = slot + base
            a, b = a.reshape(nd, band, lanes), b.reshape(nd, band, lanes)
            if add:
                a, b = a + o_ref[:, slot], b + o_ref[:, slot + 1]
            o_ref[:, slot] = a
            o_ref[:, slot + 1] = b

        @pl.when(t == 0)
        def _():
            put(0, mx * re, mx * im)

        @pl.when(t == 1)
        def _():
            put(0, my * re, my * im, True)
            put(2, mx * re, mx * im)

        @pl.when(t == 2)
        def _():
            put(2, my * re, my * im, True)

        for k in range(3):
            @pl.when(t == 3 + k)
            def _():
                put(4 + 2 * k, re, im)


def whole(shape):
    return pl.BlockSpec(shape, lambda t: (0,) * len(shape))


def forward(h, strain, lt, m2, fx, fy, devices, more):
    ny, nx = lt.shape
    shape = (devices, 20, ny // 2 // devices, nx // 4)
    shapes = [shape, (ny, nx)] if h == 0 else [shape]

    def comp(t):
        c = jnp.where(t == 1, 5, jnp.where(t == 2, 1, jnp.where(t >= 3, 7 - t, 0)))
        return (c, 0, 0)

    return pl.pallas_call(
        functools.partial(forward_kernel, h),
        grid=(6,),
        in_specs=[pl.BlockSpec((1, ny, nx), comp), whole((ny, nx)), whole((ny, nx))]
        + [whole(v.shape) for v in (fx, fy) + more],
        out_specs=[whole(v) for v in shapes],
        out_shape=[jax.ShapeDtypeStruct(v, F32) for v in shapes],
        scratch_shapes=[pltpu.VMEM((ny, nx), F32)],
        compiler_params=pltpu.CompilerParams(vmem_limit_bytes=LIMIT),
        cost_estimate=pl.CostEstimate(
            flops=6 * 3 * 2 * (ny * nx * nx // 4 + ny * ny * nx // 2),
            bytes_accessed=14 * 1024 * 1024,
            transcendentals=0,
        ),
    )(strain, lt, m2, fx, fy, *more)


def fft(re, im, sign):
    n = len(re)
    if n == 1:
        return re, im
    half = n // 2
    sr = [re[k] + re[k + half] for k in range(half)]
    si = [im[k] + im[k + half] for k in range(half)]
    dr, di = [], []
    for k in range(half):
        a, b = re[k] - re[k + half], im[k] - im[k + half]
        if k == 0:
            dr.append(a)
            di.append(b)
        elif 4 * k == n:
            dr.append(-sign * b)
            di.append(sign * a)
        else:
            c = math.cos(2.0 * math.pi * k / n)
            s = sign * math.sin(2.0 * math.pi * k / n)
            dr.append(a * c - b * s)
            di.append(a * s + b * c)
    er, ei = fft(sr, si, sign)
    orr, oi = fft(dr, di, sign)
    outr, outi = [None] * n, [None] * n
    outr[0::2], outr[1::2], outi[0::2], outi[1::2] = er, orr, ei, oi
    return outr, outi


def green_kernel(h, x_ref, my_ref, o_ref, v_ref):
    depth, _, band, lanes = x_ref.shape

    def transform(src, dst, sign):
        def body(c, carry):
            re = [src[k, 2 * c] for k in range(depth)]
            im = [src[k, 2 * c + 1] for k in range(depth)]
            re, im = fft(re, im, sign)
            for k in range(depth):
                dst[k, 2 * c] = re[k]
                dst[k, 2 * c + 1] = im[k]
            return carry

        lax.fori_loop(0, x_ref.shape[1] // 2, body, 0)

    transform(x_ref, v_ref, -1.0)
    mx = (2 * lax.broadcasted_iota(jnp.int32, (band, lanes), 1) + h).astype(F32)

    def body(k, carry):
        mz = jnp.where(k < depth // 2, k, k - depth).astype(F32)
        for g in range(2):
            my = my_ref[g]
            k2 = mx * mx + my * my + mz * mz
            live = k2 > 0.5
            inv = jnp.where(live, 1.0 / jnp.where(live, k2, 1.0), 0.0)
            for part in range(2):
                at = 10 * g + part
                wx, wy, txz, tyz, tzz = [v_ref[k, at + 2 * c] for c in range(5)]
                vx = wx + mz * txz
                vy = wy + mz * tyz
                vz = mx * txz + my * tyz + mz * tzz
                inner = (mx * vx + my * vy + mz * vz) * (coupling * inv)
                ux = (vx - mx * inner) * inv
                uy = (vy - my * inner) * inv
                uz = (vz - mz * inner) * inv
                v_ref[k, at] = ux
                v_ref[k, at + 2] = uy
                v_ref[k, at + 4] = 0.5 * (mx * uz + mz * ux)
                v_ref[k, at + 6] = 0.5 * (my * uz + mz * uy)
                v_ref[k, at + 8] = mz * uz
        return carry

    lax.fori_loop(0, depth, body, 0)
    transform(v_ref, o_ref, 1.0)


def green(h, chunk, ny):
    depth, _, band, lanes = chunk.shape
    row = 2 * (lax.axis_index("gz") * band + jnp.arange(band, dtype=jnp.int32))
    row = row[None] + jnp.arange(2, dtype=jnp.int32)[:, None]
    my = jnp.where(row < ny // 2, row, row - ny).astype(F32)
    my = jnp.broadcast_to(my[:, :, None], (2, band, lanes))
    return pl.pallas_call(
        functools.partial(green_kernel, h),
        in_specs=[pl.BlockSpec(memory_space=pltpu.VMEM)] * 2,
        out_specs=pl.BlockSpec(memory_space=pltpu.VMEM),
        out_shape=jax.ShapeDtypeStruct(chunk.shape, F32),
        scratch_shapes=[pltpu.VMEM(chunk.shape, F32)],
        compiler_params=pltpu.CompilerParams(vmem_limit_bytes=LIMIT),
        cost_estimate=pl.CostEstimate(
            flops=chunk.size * 64, bytes_accessed=chunk.size * 8, transcendentals=0
        ),
    )(chunk, my)


def inverse_kernel(h, r_ref, x_ref, y_ref, *rest):
    g_ref = rest[-1]
    t = pl.program_id(0)
    lanes = r_ref.shape[3]
    hy = r_ref.shape[0] * r_ref.shape[2]
    sums = []
    for g in range(2):
        mx, my = waves((h, g), 2 * hy, lanes)

        def get(slot, base=10 * g):
            slot = slot + base
            return [r_ref[:, slot + part].reshape(hy, lanes) for part in range(2)]

        def put(a, b):
            g_ref[:, :lanes] = a
            g_ref[:, lanes:] = b

        @pl.when(t == 0)
        def _():
            a, b = get(0)
            put(mx * a, mx * b)

        @pl.when(t == 1)
        def _():
            a, b = get(2)
            put(my * a, my * b)

        @pl.when(t == 5)
        def _():
            a, b = get(0)
            c, d = get(2)
            put(0.5 * (my * a + mx * c), 0.5 * (my * b + mx * d))

        @pl.when((t >= 2) & (t <= 4))
        def _():
            put(*get(2 * (6 - t)))

        d = dot_left(y_ref[g], g_ref[...])
        re = d[:hy, :lanes] - d[hy:, lanes:]
        im = d[:hy, lanes:] + d[hy:, :lanes]
        sums.append(jnp.concatenate([re, im], axis=1))
    full = jnp.concatenate([sums[0] + sums[1], sums[0] - sums[1]], axis=0)
    z = dot_right(full, x_ref[...])
    if h == 0:
        rest[0][0] = z
    else:
        z0_ref, e_ref, o_ref = rest[:3]
        hx = z.shape[1]
        z0 = z0_ref[0]
        o_ref[0, :, :hx] = e_ref[0, :, :hx] - (z0 + z)
        o_ref[0, :, hx:] = e_ref[0, :, hx:] - (z0 - z)


def inverse(h, r, ix, iy, ny, nx, extra=()):
    def plane(width):
        return pl.BlockSpec((1, ny, width), lambda t: (t, 0, 0))

    width = nx // 2 if h == 0 else nx
    return pl.pallas_call(
        functools.partial(inverse_kernel, h),
        grid=(6,),
        in_specs=[whole(v.shape) for v in (r, ix, iy)]
        + [plane(v.shape[2]) for v in extra],
        out_specs=plane(width),
        out_shape=jax.ShapeDtypeStruct((6, ny, width), F32),
        scratch_shapes=[pltpu.VMEM((ny // 2, nx // 2), F32)],
        compiler_params=pltpu.CompilerParams(vmem_limit_bytes=LIMIT),
        cost_estimate=pl.CostEstimate(
            flops=6 * 3 * 2 * (ny * nx * nx // 4 + ny * ny * nx // 2),
            bytes_accessed=14 * 1024 * 1024,
            transcendentals=0,
        ),
    )(r, ix, iy, *extra)


def shards(
    order_param,
    concentration,
    strain,
    grain_ids,
    seed_labels,
    grain_moduli,
    grain_mobility,
    seed_rate,
):
    devices = lax.axis_size("gz")
    ny, nx = strain.shape[2], strain.shape[3]
    fx, fy, ix, iy = tables(nx, ny, devices)
    fx, ix = [[triple(v, 0, (0, 1, 0)) for v in w] for w in (fx, ix)]
    fy, iy = [triple(v, 2, (0, 1, 0)) for v in (fy, iy)]
    strain = strain.reshape(6, ny, nx)
    p, c = order_param[0], concentration[0]
    p_halo = neighbours(p)
    c_halo = neighbours(c)
    lt, m2, kinetic, decay, p_part, c_part = planes_call(
        local_kernel,
        (grain_moduli, grain_mobility, seed_rate),
        (p, c, strain, grain_ids[0], seed_labels[0]),
        6,
    )
    p1 = p_part + kinetic * (p_halo[0] + p_halo[1])
    p1_halo = neighbours(p1)
    c1, p2_part, c2_part = planes_call(
        second_kernel, (), (p1, c_part, *c_halo, kinetic, decay), 3
    )

    p1_halo, c1 = lax.optimization_barrier((p1_halo, c1))
    c1_halo = neighbours(c1)

    def swap(chunk):
        return lax.all_to_all(chunk, "gz", split_axis=0, concat_axis=0, tiled=True)

    sent0, p2 = forward(0, strain, lt, m2, fx[0], fy, devices, (p2_part, kinetic, *p1_halo))
    (sent1,) = forward(1, strain, lt, m2, fx[1], fy, devices, (p2,))
    band0 = swap(sent0)
    sent1, c1_halo = lax.optimization_barrier((sent1, c1_halo))
    c2 = c2_part + time_step * (c1_halo[0] + c1_halo[1]) - p2
    band1 = swap(sent1)
    done0, band1 = lax.optimization_barrier((green(0, band0, ny), band1))
    back0 = swap(done0)
    back1 = swap(green(1, band1, ny))
    z0 = inverse(0, back0, ix[0], iy, ny, nx)
    out = inverse(1, back1, ix[1], iy, ny, nx, (z0, strain))
    return (p2[None], c2[None], out[:, None])


def solution(mesh):
    return jax.shard_map(
        shards,
        mesh=mesh,
        in_specs=(
            P("gz", None, None),
            P("gz", None, None),
            P(None, "gz", None, None),
            P("gz", None, None),
            P("gz", None, None),
            P(),
            P(),
            P(),
        ),
        out_specs=(P("gz", None, None), P("gz", None, None), P(None, "gz", None, None)),
        check_vma=False,
    )
```

```python
import functools
import math

import jax
import jax.numpy as jnp
import ml_dtypes
import numpy as np
from jax import lax
from jax.experimental import pallas as pl
from jax.experimental.pallas import tpu as pltpu
from jax.sharding import PartitionSpec as P

SUBSTEPS = 2
time_step = 0.05
conc_eq = 0.5
residual_stiff = 0.1
lame_ref = 1.0
shear_ref = 1.0
coupling = (lame_ref + shear_ref) / (shear_ref * (lame_ref + 2.0 * shear_ref))
F32 = jnp.float32
BF16 = jnp.bfloat16
LIMIT = 50 * 1024 * 1024


def neighbours(plane):
    count = lax.axis_size("gz")
    below = lax.ppermute(plane, "gz", [(i, (i + 1) % count) for i in range(count)])
    above = lax.ppermute(plane, "gz", [((i + 1) % count, i) for i in range(count)])
    return below, above


def laplace_plane(plane):
    ny, nx = plane.shape
    y_sum = pltpu.roll(plane, 1, 0) + pltpu.roll(plane, ny - 1, 0)
    x_sum = pltpu.roll(plane, 1, 1) + pltpu.roll(plane, nx - 1, 1)
    return y_sum + x_sum - 6.0 * plane


def order_part(p, c, kinetic, decay):
    well = 2.0 * p * (1.0 - p) * (1.0 - 2.0 * p)
    interp = 6.0 * p * (1.0 - p)
    force = laplace_plane(p) - well + 2.0 * interp * (c - conc_eq)
    return p + kinetic * force - decay * p


def local_kernel(
    moduli_ref, mobility_ref, rate_ref, p_ref, c_ref, e_ref, ids_ref, seeds_ref,
    lt_ref, m2_ref, kin_ref, dec_ref, pa_ref, ca_ref,
):
    rows = 8

    def body(k, carry):
        at = pl.ds(pl.multiple_of(k * rows, rows), rows)
        ids, seeds = ids_ref[at, :], seeds_ref[at, :]
        lame = jnp.zeros(ids.shape, F32)
        shear, mobility, rate = lame, lame, lame
        for n in range(mobility_ref.shape[0]):
            hit = ids == n
            lame = jnp.where(hit, moduli_ref[0, n], lame)
            shear = jnp.where(hit, moduli_ref[1, n], shear)
            mobility = jnp.where(hit, mobility_ref[n], mobility)
        for n in range(rate_ref.shape[0]):
            rate = jnp.where(seeds == n + 1, rate_ref[n], rate)
        e = [e_ref[n, at, :] for n in range(6)]
        trace = e[0] + e[1] + e[2]
        square = (
            e[0] * e[0] + e[1] * e[1] + e[2] * e[2]
            + 2.0 * (e[3] * e[3] + e[4] * e[4] + e[5] * e[5])
        )
        energy = 0.5 * lame * trace * trace + shear * square
        kin_ref[at, :] = time_step * mobility * (1.0 + energy / (1.0 + energy))
        dec_ref[at, :] = time_step * rate
        lt_ref[at, :] = lame * trace
        m2_ref[at, :] = 2.0 * shear
        return carry

    lax.fori_loop(0, p_ref.shape[0] // rows, body, 0)
    p, c = p_ref[...], c_ref[...]
    pa_ref[...] = order_part(p, c, kin_ref[...], dec_ref[...])
    ca_ref[...] = c + time_step * laplace_plane(c) + p


def second_kernel(p1_ref, ca_ref, cb_ref, cu_ref, kin_ref, dec_ref, c1_ref, pa_ref, cc_ref):
    p1 = p1_ref[...]
    c1_ref[...] = ca_ref[...] + time_step * (cb_ref[...] + cu_ref[...]) - p1
    pa_ref[...] = order_part(p1, c1_ref[...], kin_ref[...], dec_ref[...])
    c1 = c1_ref[...]
    cc_ref[...] = c1 + time_step * laplace_plane(c1) + p1


def planes_call(kernel, scalars, arrays, outs):
    shape = arrays[0].shape
    total = sum(v.size * 4 for v in arrays) + outs * 4 * arrays[0].size
    return pl.pallas_call(
        kernel,
        in_specs=[pl.BlockSpec(memory_space=pltpu.SMEM)] * len(scalars)
        + [pl.BlockSpec(memory_space=pltpu.VMEM)] * len(arrays),
        out_specs=[pl.BlockSpec(memory_space=pltpu.VMEM)] * outs,
        out_shape=[jax.ShapeDtypeStruct(shape, F32)] * outs,
        compiler_params=pltpu.CompilerParams(vmem_limit_bytes=LIMIT),
        cost_estimate=pl.CostEstimate(flops=100 * total, bytes_accessed=total, transcendentals=0),
    )(*scalars, *arrays)


def parts(table, axis, order):
    table = np.asarray(table, np.float32)
    hi = table.astype(ml_dtypes.bfloat16)
    lo = (table - hi.astype(np.float32)).astype(ml_dtypes.bfloat16)
    return jnp.asarray(np.concatenate([(hi, lo)[k] for k in order], axis=axis))


def tables(nx, ny, depth):
    hx, hy = nx // 2, ny // 2
    x = np.arange(hx)[:, None]
    y = np.arange(hy)[None, :]
    fx, ix, fy, iy = [], [], [], []
    for par in range(2):
        kx = 2 * np.arange(hx // 2)[None, :] + par
        ph = 2.0 * np.pi * ((x * kx) % nx) / nx
        fx.append(np.concatenate([np.cos(ph), -np.sin(ph)], 1))
        weight = np.where(kx == 0, 1.0, 2.0) / float(nx * ny * depth)
        ix.append(np.concatenate([np.cos(ph) * weight, -np.sin(ph) * weight], 1).T)
        ky = 2 * np.arange(hy)[:, None] + par
        ph = 2.0 * np.pi * ((ky * y) % ny) / ny
        fy.append(np.concatenate([np.cos(ph), np.sin(ph)], 0))
        iy.append(np.concatenate([np.cos(ph).T, np.sin(ph).T], 0))
    return fx, np.stack(fy), ix, np.stack(iy)


def split(x):
    hi = x.astype(BF16)
    return hi, (x - hi.astype(F32)).astype(BF16)


def dot(u, v):
    return jnp.dot(u, v, preferred_element_type=F32)


def dot_right(a, table):
    hi, lo = split(a)
    n = table.shape[0] // 2
    return dot(hi, table[:n]) + (dot(hi, table[n:]) + dot(lo, table[:n]))


def dot_left(table, b):
    hi, lo = split(b)
    n = table.shape[1] // 2
    return dot(table[:, :n], hi) + (dot(table[:, n:], hi) + dot(table[:, :n], lo))


def waves(par, ny, lanes):
    mx = (2 * lax.broadcasted_iota(jnp.int32, (1, lanes), 1) + par[0]).astype(F32)
    row = 2 * lax.broadcasted_iota(jnp.int32, (ny // 2, 1), 0) + par[1]
    my = jnp.where(row < ny // 2, row, row - ny).astype(F32)
    return mx, my


def forward_kernel(h, e_ref, lt_ref, m2_ref, x_ref, y_ref, *rest):
    t = pl.program_id(0)
    scale_ref = rest[-1]

    @pl.when(t == 0)
    def _():
        if h == 0:
            pa_ref, kin_ref, pb_ref, pu_ref, _, p_ref, _ = rest
            p_ref[...] = pa_ref[...] + kin_ref[...] * (pb_ref[...] + pu_ref[...])
        else:
            p_ref = rest[0]
        p = p_ref[...]
        scale_ref[...] = p * p * (3.0 - 2.0 * p) + residual_stiff

    o_ref = rest[4] if h == 0 else rest[1]
    nd, _, band, _ = o_ref.shape
    ny, nx = lt_ref.shape
    hy, hx, lanes = ny // 2, nx // 2, nx // 4
    diag = jnp.where((t == 0) | (t == 2) | (t == 5), 1.0, 0.0).astype(F32)
    s = scale_ref[...] * (m2_ref[...] * e_ref[0] + diag * lt_ref[...])
    left, right = s[:, :hx], s[:, hx:]
    folded = left + right if h == 0 else left - right
    xs = dot_right(folded, x_ref[...])
    for g in range(2):
        ys = xs[:hy] + xs[hy:] if g == 0 else xs[:hy] - xs[hy:]
        d = dot_left(y_ref[g], ys)
        re = d[:hy, :lanes] + d[hy:, lanes:]
        im = d[:hy, lanes:] - d[hy:, :lanes]
        mx, my = waves((h, g), ny, lanes)

        def put(slot, a, b, add=False, base=10 * g):
            slot = slot + base
            a, b = a.reshape(nd, band, lanes), b.reshape(nd, band, lanes)
            if add:
                a, b = a + o_ref[:, slot], b + o_ref[:, slot + 1]
            o_ref[:, slot] = a
            o_ref[:, slot + 1] = b

        @pl.when(t == 0)
        def _():
            put(0, mx * re, mx * im)

        @pl.when(t == 1)
        def _():
            put(0, my * re, my * im, True)
            put(2, mx * re, mx * im)

        @pl.when(t == 2)
        def _():
            put(2, my * re, my * im, True)

        for k in range(3):
            @pl.when(t == 3 + k)
            def _():
                put(4 + 2 * k, re, im)


def whole(shape):
    return pl.BlockSpec(shape, lambda t: (0,) * len(shape))


def forward(h, strain, lt, m2, fx, fy, devices, more):
    ny, nx = lt.shape
    shape = (devices, 20, ny // 2 // devices, nx // 4)
    shapes = [shape, (ny, nx)] if h == 0 else [shape]

    def comp(t):
        c = jnp.where(t == 1, 5, jnp.where(t == 2, 1, jnp.where(t >= 3, 7 - t, 0)))
        return (c, 0, 0)

    return pl.pallas_call(
        functools.partial(forward_kernel, h),
        grid=(6,),
        in_specs=[pl.BlockSpec((1, ny, nx), comp), whole((ny, nx)), whole((ny, nx))]
        + [whole(v.shape) for v in (fx, fy) + more],
        out_specs=[whole(v) for v in shapes],
        out_shape=[jax.ShapeDtypeStruct(v, F32) for v in shapes],
        scratch_shapes=[pltpu.VMEM((ny, nx), F32)],
        compiler_params=pltpu.CompilerParams(vmem_limit_bytes=LIMIT),
        cost_estimate=pl.CostEstimate(
            flops=6 * 3 * 2 * (ny * nx * nx // 4 + ny * ny * nx // 2),
            bytes_accessed=14 * 1024 * 1024,
            transcendentals=0,
        ),
    )(strain, lt, m2, fx, fy, *more)


def fft(re, im, sign):
    n = len(re)
    if n == 1:
        return re, im
    half = n // 2
    sr = [re[k] + re[k + half] for k in range(half)]
    si = [im[k] + im[k + half] for k in range(half)]
    dr, di = [], []
    for k in range(half):
        a, b = re[k] - re[k + half], im[k] - im[k + half]
        if k == 0:
            dr.append(a)
            di.append(b)
        elif 4 * k == n:
            dr.append(-sign * b)
            di.append(sign * a)
        else:
            c = math.cos(2.0 * math.pi * k / n)
            s = sign * math.sin(2.0 * math.pi * k / n)
            dr.append(a * c - b * s)
            di.append(a * s + b * c)
    er, ei = fft(sr, si, sign)
    orr, oi = fft(dr, di, sign)
    outr, outi = [None] * n, [None] * n
    outr[0::2], outr[1::2], outi[0::2], outi[1::2] = er, orr, ei, oi
    return outr, outi


def green_kernel(h, x_ref, my_ref, o_ref, v_ref):
    depth, _, band, lanes = x_ref.shape

    def transform(src, dst, sign):
        def body(c, carry):
            re = [src[k, 2 * c] for k in range(depth)]
            im = [src[k, 2 * c + 1] for k in range(depth)]
            re, im = fft(re, im, sign)
            for k in range(depth):
                dst[k, 2 * c] = re[k]
                dst[k, 2 * c + 1] = im[k]
            return carry

        lax.fori_loop(0, x_ref.shape[1] // 2, body, 0)

    transform(x_ref, v_ref, -1.0)
    mx = (2 * lax.broadcasted_iota(jnp.int32, (band, lanes), 1) + h).astype(F32)

    def body(k, carry):
        mz = jnp.where(k < depth // 2, k, k - depth).astype(F32)
        for g in range(2):
            my = my_ref[g]
            k2 = mx * mx + my * my + mz * mz
            live = k2 > 0.5
            inv = jnp.where(live, 1.0 / jnp.where(live, k2, 1.0), 0.0)
            for part in range(2):
                at = 10 * g + part
                wx, wy, txz, tyz, tzz = [v_ref[k, at + 2 * c] for c in range(5)]
                vx = wx + mz * txz
                vy = wy + mz * tyz
                vz = mx * txz + my * tyz + mz * tzz
                inner = (mx * vx + my * vy + mz * vz) * (coupling * inv)
                ux = (vx - mx * inner) * inv
                uy = (vy - my * inner) * inv
                uz = (vz - mz * inner) * inv
                v_ref[k, at] = ux
                v_ref[k, at + 2] = uy
                v_ref[k, at + 4] = 0.5 * (mx * uz + mz * ux)
                v_ref[k, at + 6] = 0.5 * (my * uz + mz * uy)
                v_ref[k, at + 8] = mz * uz
        return carry

    lax.fori_loop(0, depth, body, 0)
    transform(v_ref, o_ref, 1.0)


def green(h, chunk, ny):
    depth, _, band, lanes = chunk.shape
    row = 2 * (lax.axis_index("gz") * band + jnp.arange(band, dtype=jnp.int32))
    row = row[None] + jnp.arange(2, dtype=jnp.int32)[:, None]
    my = jnp.where(row < ny // 2, row, row - ny).astype(F32)
    my = jnp.broadcast_to(my[:, :, None], (2, band, lanes))
    return pl.pallas_call(
        functools.partial(green_kernel, h),
        in_specs=[pl.BlockSpec(memory_space=pltpu.VMEM)] * 2,
        out_specs=pl.BlockSpec(memory_space=pltpu.VMEM),
        out_shape=jax.ShapeDtypeStruct(chunk.shape, F32),
        scratch_shapes=[pltpu.VMEM(chunk.shape, F32)],
        compiler_params=pltpu.CompilerParams(vmem_limit_bytes=LIMIT),
        cost_estimate=pl.CostEstimate(
            flops=chunk.size * 64, bytes_accessed=chunk.size * 8, transcendentals=0
        ),
    )(chunk, my)


def inverse_kernel(h, r_ref, x_ref, y_ref, *rest):
    g_ref = rest[-1]
    t = pl.program_id(0)
    lanes = r_ref.shape[3]
    hy = r_ref.shape[0] * r_ref.shape[2]
    sums = []
    for g in range(2):
        mx, my = waves((h, g), 2 * hy, lanes)

        def get(slot, base=10 * g):
            slot = slot + base
            return [r_ref[:, slot + part].reshape(hy, lanes) for part in range(2)]

        def put(a, b):
            g_ref[:, :lanes] = a
            g_ref[:, lanes:] = b

        @pl.when(t == 0)
        def _():
            a, b = get(0)
            put(mx * a, mx * b)

        @pl.when(t == 1)
        def _():
            a, b = get(2)
            put(my * a, my * b)

        @pl.when(t == 5)
        def _():
            a, b = get(0)
            c, d = get(2)
            put(0.5 * (my * a + mx * c), 0.5 * (my * b + mx * d))

        @pl.when((t >= 2) & (t <= 4))
        def _():
            put(*get(2 * (6 - t)))

        d = dot_left(y_ref[g], g_ref[...])
        re = d[:hy, :lanes] - d[hy:, lanes:]
        im = d[:hy, lanes:] + d[hy:, :lanes]
        sums.append(jnp.concatenate([re, im], axis=1))
    full = jnp.concatenate([sums[0] + sums[1], sums[0] - sums[1]], axis=0)
    z = dot_right(full, x_ref[...])
    if h == 0:
        rest[0][0] = z
    else:
        z0_ref, e_ref, o_ref = rest[:3]
        hx = z.shape[1]
        z0 = z0_ref[0]
        o_ref[0, :, :hx] = e_ref[0, :, :hx] - (z0 + z)
        o_ref[0, :, hx:] = e_ref[0, :, hx:] - (z0 - z)


def inverse(h, r, ix, iy, ny, nx, extra=()):
    def plane(width):
        return pl.BlockSpec((1, ny, width), lambda t: (t, 0, 0))

    width = nx // 2 if h == 0 else nx
    return pl.pallas_call(
        functools.partial(inverse_kernel, h),
        grid=(6,),
        in_specs=[whole(v.shape) for v in (r, ix, iy)]
        + [plane(v.shape[2]) for v in extra],
        out_specs=plane(width),
        out_shape=jax.ShapeDtypeStruct((6, ny, width), F32),
        scratch_shapes=[pltpu.VMEM((ny // 2, nx // 2), F32)],
        compiler_params=pltpu.CompilerParams(vmem_limit_bytes=LIMIT),
        cost_estimate=pl.CostEstimate(
            flops=6 * 3 * 2 * (ny * nx * nx // 4 + ny * ny * nx // 2),
            bytes_accessed=14 * 1024 * 1024,
            transcendentals=0,
        ),
    )(r, ix, iy, *extra)


def shards(
    order_param,
    concentration,
    strain,
    grain_ids,
    seed_labels,
    grain_moduli,
    grain_mobility,
    seed_rate,
):
    devices = lax.axis_size("gz")
    ny, nx = strain.shape[2], strain.shape[3]
    fx, fy, ix, iy = tables(nx, ny, devices)
    fx, ix = [[parts(v, 0, (0, 1)) for v in w] for w in (fx, ix)]
    fy, iy = [parts(v, 2, (0, 1)) for v in (fy, iy)]
    strain = strain.reshape(6, ny, nx)
    p, c = order_param[0], concentration[0]
    p_halo = neighbours(p)
    c_halo = neighbours(c)
    lt, m2, kinetic, decay, p_part, c_part = planes_call(
        local_kernel,
        (grain_moduli, grain_mobility, seed_rate),
        (p, c, strain, grain_ids[0], seed_labels[0]),
        6,
    )
    p1 = p_part + kinetic * (p_halo[0] + p_halo[1])
    p1_halo = neighbours(p1)
    c1, p2_part, c2_part = planes_call(
        second_kernel, (), (p1, c_part, *c_halo, kinetic, decay), 3
    )

    p1_halo, c1 = lax.optimization_barrier((p1_halo, c1))
    c1_halo = neighbours(c1)

    def swap(chunk):
        return lax.all_to_all(chunk, "gz", split_axis=0, concat_axis=0, tiled=True)

    sent0, p2 = forward(0, strain, lt, m2, fx[0], fy, devices, (p2_part, kinetic, *p1_halo))
    (sent1,) = forward(1, strain, lt, m2, fx[1], fy, devices, (p2,))
    sent0, c1_halo = lax.optimization_barrier((sent0, c1_halo))
    band0 = swap(sent0)
    c2 = c2_part + time_step * (c1_halo[0] + c1_halo[1]) - p2
    band1 = swap(sent1)
    done0, band1 = lax.optimization_barrier((green(0, band0, ny), band1))
    back0 = swap(done0)
    back1 = swap(green(1, band1, ny))
    z0 = inverse(0, back0, ix[0], iy, ny, nx)
    out = inverse(1, back1, ix[1], iy, ny, nx, (z0, strain))
    return (p2[None], c2[None], out[:, None])


def solution(mesh):
    return jax.shard_map(
        shards,
        mesh=mesh,
        in_specs=(
            P("gz", None, None),
            P("gz", None, None),
            P(None, "gz", None, None),
            P("gz", None, None),
            P("gz", None, None),
            P(),
            P(),
            P(),
        ),
        out_specs=(P("gz", None, None), P("gz", None, None), P(None, "gz", None, None)),
        check_vma=False,
    )
```
